256 devices in a mesh: var: 32 (over z_lo, x, core), tp: 8 (over z_hi, y).
Axes of the slice: x: 4, y: 4, z: 8 (z_hi: 2, z_lo: 4; z = z_hi * 4 + z_lo), core: 2. Of those that a mesh axis runs over, the one named last changes fastest.
Arguments:
- parent_inputs: bfloat16 [4096, 256], P('var'), may hold values from -6 to 6
- gate_parent: bfloat16 [4096, 7168], P('var', 'tp'), may hold values from -0.09375 to 0.09375
- up_parent: bfloat16 [4096, 7168], P('var', 'tp'), may hold values from -0.09375 to 0.09375
- down_parent: bfloat16 [7168, 4096], P('tp', 'var'), may hold values from -0.0625 to 0.0625
- targets: bfloat16 [256, 4096], P('var', 'tp'), may hold values from -6 to 6
- widths: int32 [32], P('var'), may hold values from 1792 to 7168, as said below
- gains: float32 [32, 7168], P('var', 'tp'), may hold values from 0.25 to 2
Outputs:
- down_grad: bfloat16 [32, 7168, 4096], P('var', 'tp')
- gain_grad: float32 [32, 7168], P('var', 'tp')
The draws below stay inside these ranges and needn't reach their ends.
Inputs may be any that keep to these rules, and one draw needn't show every extreme that they name: `widths`: every draw has a variant of exactly 7168 and one of exactly 1792 kept hidden units.
All inputs are finite; a program needn't handle non-finite values.
Results may differ from the reference program's by a relative error of at most 0.0059.
Values may be sent and summed in bfloat16 or wider, within the bound.
No kernel may reach another device: no remote copies, remote signals or barrier semaphores. Data moves between devices by JAX's collectives and lax.ppermute only.
A program may use at most 128 MiB of HBM per device.

```python
import math
import jax
import jax.numpy as jnp
from jax import lax

D = 4096
FF_MAX = 7168
ROWS = 256
VARIANTS = 32


def draw_widths(key, part):
    key = jax.random.fold_in(key, 11)
    first, second, third = jax.random.split(key, 3)
    base = jax.random.randint(first, (VARIANTS,), FF_MAX // 4, FF_MAX + 1)
    widest = jax.random.randint(second, (), 0, VARIANTS)
    narrowest = (widest + 1 + jax.random.randint(third, (), 0, VARIANTS - 1)) % VARIANTS
    places = jnp.arange(VARIANTS, dtype=jnp.int32)
    base = jnp.where(places == widest, FF_MAX, base)
    base = jnp.where(places == narrowest, FF_MAX // 4, base)
    return base.astype(jnp.int32)


def steps_of(own_key, extent, cuts, low, top_value):
    loudness, own = 1.0, jax.random.fold_in(own_key, 6)
    for axis_at, parts in cuts:
        steps = jnp.exp(jax.random.uniform(jax.random.fold_in(own, axis_at), (parts,), jnp.float32, low / len(cuts), top_value / len(cuts)))
        loudness = loudness * jnp.repeat(steps, extent[axis_at] // parts).reshape([-1 if axis == axis_at else 1 for axis in range(len(extent))])
    return loudness


def gaussian(stream_key, dims, scale, limit, cuts=(), kind=jnp.bfloat16):
    factor_of = steps_of(stream_key, dims, cuts, -0.22, 0.18) if cuts else 1.0
    drawn = jax.random.normal(stream_key, dims, jnp.float32) * scale * factor_of
    return jnp.minimum(jnp.maximum(drawn, -limit), limit).astype(kind)


def setup_inputs(seed: int = 0) -> dict:
    key_list = jax.random.split(jax.random.key(seed), 8)
    return {
        "parent_inputs": gaussian(key_list[0], (D, ROWS), 1.0, 6.0, ((0, 32),)),
        "gate_parent": gaussian(key_list[1], (D, FF_MAX), D ** -0.5, 0.09375, ((0, 32), (1, 8))),
        "up_parent": gaussian(key_list[2], (D, FF_MAX), D ** -0.5, 0.09375, ((0, 32), (1, 8))),
        "down_parent": gaussian(key_list[3], (FF_MAX, D), FF_MAX ** -0.5, 0.0625, ((0, 8), (1, 32))),
        "targets": gaussian(key_list[4], (ROWS, D), 1.0, 6.0, ((0, 32), (1, 8))),
        "widths": draw_widths(jax.random.fold_in(key_list[7], 71), 0),
        "gains": jnp.clip(jnp.exp(math.log(2.0) - 2.0794415 * jax.random.uniform(key_list[6], (VARIANTS, FF_MAX), jnp.float32) ** steps_of(key_list[6], (VARIANTS, FF_MAX), ((0, 32), (1, 8)), -0.2, 0.2)), 0.25, 2.0),
    }


def reference(parent_inputs, gate_parent, up_parent, down_parent, targets, widths, gains):
    contract_rows = (((0,), (0,)), ((), ()))
    gate = lax.dot_general(parent_inputs, gate_parent, contract_rows, preferred_element_type=jnp.float32)
    up = lax.dot_general(parent_inputs, up_parent, contract_rows, preferred_element_type=jnp.float32)
    raw = jax.nn.silu(gate) * up
    column = jnp.arange(FF_MAX, dtype=jnp.int32)
    scale = 1.0 / (ROWS ** 0.5)
    target = targets.astype(jnp.float32)

    def one_variant(pair):
        width, gain = pair
        kept = (column < width).astype(jnp.float32)
        hidden = (raw * gain * kept).astype(jnp.bfloat16)
        output = jnp.dot(hidden, down_parent, preferred_element_type=jnp.float32)
        residual = (output - target).astype(jnp.bfloat16)
        grad_down = lax.dot_general(hidden, residual, contract_rows, preferred_element_type=jnp.float32)
        grad_down = (grad_down * scale).astype(jnp.bfloat16)
        back = lax.dot_general(residual, down_parent, (((1,), (1,)), ((), ())), preferred_element_type=jnp.float32)
        grad_gain = kept * jnp.sum(raw * back, axis=0) * scale
        return grad_down, grad_gain

    down_grad, gain_grad = lax.map(one_variant, (widths, gains))
    return down_grad, gain_grad
```

```python
import functools

import jax
import jax.numpy as jnp
from jax import lax
from jax.experimental import pallas as pl
from jax.experimental.pallas import tpu as pltpu
from jax.sharding import Mesh, PartitionSpec as P

SHAPE = (4, 4, 2, 2, 4)
AXES = ("zl", "x", "core", "zh", "y")
VAR = ("zl", "x", "core")
SIZE = dict(zip(AXES, SHAPE))
MIB = 1024 * 1024


def swap(value, axis, mask=1):
    return lax.ppermute(value, axis, [(i, i ^ mask) for i in range(SIZE[axis])])


def pick(stacked, places, axis=0):
    return jnp.stack([lax.dynamic_index_in_dim(stacked, p, axis, keepdims=False) for p in places], axis)


def gather4(value, axis):
    me = lax.axis_index(axis)
    near = jnp.stack([value] + [swap(value, axis, k) for k in (1, 2, 3)])
    return pick(near, [me ^ a for a in range(4)])


def gather_pair(value):
    other = swap(value, "core")
    first = lax.axis_index("core") == 0
    return jnp.stack([jnp.where(first, value, other), jnp.where(first, other, value)])


def gather_tp(value):
    far = swap(value, "zh")
    return [value] + [swap(value, "y", k) for k in (1, 2, 3)] + [far] + [swap(far, "y", k) for k in (1, 2, 3)]


def output_kernel(raw_ref, gain_ref, down_ref, target_ref, res_ref, hidden, total):
    step = pl.program_id(0)
    variants = gain_ref.shape[1]
    rows = raw_ref.shape[1]
    raw = raw_ref[0]
    for v in range(variants):
        hidden[v * rows : (v + 1) * rows, :] = (raw * gain_ref[0, v : v + 1, :]).astype(jnp.bfloat16)
    term = jnp.dot(hidden[...], down_ref[0], preferred_element_type=jnp.float32)

    @pl.when(step == 0)
    def _():
        total[...] = term

    @pl.when(step > 0)
    def _():
        total[...] += term

    @pl.when(step == pl.num_programs(0) - 1)
    def _():
        whole = total[...].reshape(variants, rows, total.shape[1])
        res_ref[...] = (whole - target_ref[...].astype(jnp.float32)[None]).astype(jnp.bfloat16)


def output_call(raw8, gain8, down8, target):
    pieces, rows, width = raw8.shape
    variants = gain8.shape[1]
    feats = down8.shape[2]
    return pl.pallas_call(
        output_kernel,
        grid=(pieces,),
        in_specs=[
            pl.BlockSpec((1, rows, width), lambda s: (s, 0, 0)),
            pl.BlockSpec((1, variants, width), lambda s: (s, 0, 0)),
            pl.BlockSpec((1, width, feats), lambda s: (s, 0, 0)),
            pl.BlockSpec((rows, feats), lambda s: (0, 0)),
        ],
        out_specs=pl.BlockSpec((variants, rows, feats), lambda s: (0, 0, 0)),
        out_shape=jax.ShapeDtypeStruct((variants, rows, feats), jnp.bfloat16),
        scratch_shapes=[
            pltpu.VMEM((variants * rows, width), jnp.bfloat16),
            pltpu.VMEM((variants * rows, feats), jnp.float32),
        ],
        compiler_params=pltpu.CompilerParams(vmem_limit_bytes=24 * MIB),
        cost_estimate=pl.CostEstimate(
            flops=2 * variants * rows * pieces * width * feats, bytes_accessed=4 * MIB, transcendentals=0
        ),
        name="output",
    )(raw8, gain8, down8, target)


def back_kernel(res_ref, raw_ref, down_ref, out_ref):
    variants, rows, feats = res_ref.shape
    width = raw_ref.shape[2]
    raw = raw_ref[0]
    some = 8
    for at in range(0, variants, some):
        res = res_ref[at : at + some].reshape(some * rows, feats)
        back = lax.dot_general(
            res, down_ref[0], (((1,), (1,)), ((), ())), preferred_element_type=jnp.float32
        )
        out_ref[0, at : at + some, :] = jnp.sum(back.reshape(some, rows, width) * raw[None], axis=1)


def back_call(res, raw8, down8):
    pieces, rows, width = raw8.shape
    variants, _, feats = res.shape
    return pl.pallas_call(
        back_kernel,
        grid=(pieces,),
        in_specs=[
            pl.BlockSpec((variants, rows, feats), lambda s: (0, 0, 0)),
            pl.BlockSpec((1, rows, width), lambda s: (s, 0, 0)),
            pl.BlockSpec((1, width, feats), lambda s: (s, 0, 0)),
        ],
        out_specs=pl.BlockSpec((1, variants, width), lambda s: (s, 0, 0)),
        out_shape=jax.ShapeDtypeStruct((pieces, variants, width), jnp.float32),
        compiler_params=pltpu.CompilerParams(vmem_limit_bytes=24 * MIB),
        cost_estimate=pl.CostEstimate(
            flops=2 * variants * rows * pieces * width * feats, bytes_accessed=4 * MIB, transcendentals=0
        ),
        name="back",
    )(res, raw8, down8)


def grad_kernel(scale, raw_ref, gain_ref, *refs):
    res_refs, out_ref, hidden_t, block = refs[:8], refs[8], refs[9], refs[10]
    rows = raw_ref.shape[1]
    some, feats = res_refs[0].shape[0], res_refs[0].shape[2]

    @pl.when(pl.program_id(0) == 0)
    def _():
        for p in range(8):
            hidden = (raw_ref[p] * gain_ref[...]).astype(jnp.bfloat16)
            block[p * rows : (p + 1) * rows, : hidden.shape[1]] = hidden
        hidden_t[...] = block[:, : hidden_t.shape[0]].T

    for p in range(8):
        for q in range(some):
            block[p * rows : (p + 1) * rows, q * feats : (q + 1) * feats] = res_refs[p][q]
    grad = jnp.dot(hidden_t[...], block[:, : some * feats], preferred_element_type=jnp.float32)
    out_ref[0] = (grad * scale).astype(jnp.bfloat16)


def grad_call(raw8, gain, res8, scale):
    pieces, rows, width = raw8.shape
    blocks, _, feats = res8[0].shape
    some = 4
    return pl.pallas_call(
        functools.partial(grad_kernel, scale),
        grid=(blocks // some,),
        in_specs=[
            pl.BlockSpec((pieces, rows, width), lambda s: (0, 0, 0)),
            pl.BlockSpec((1, width), lambda s: (0, 0)),
        ]
        + [pl.BlockSpec((some, rows, feats), lambda s: (s, 0, 0))] * 8,
        out_specs=pl.BlockSpec((1, width, some * feats), lambda s: (0, 0, s)),
        out_shape=jax.ShapeDtypeStruct((1, width, blocks * feats), jnp.bfloat16),
        scratch_shapes=[
            pltpu.VMEM((width, pieces * rows), jnp.bfloat16),
            pltpu.VMEM((pieces * rows, max(width, some * feats)), jnp.bfloat16),
        ],
        compiler_params=pltpu.CompilerParams(vmem_limit_bytes=24 * MIB),
        cost_estimate=pl.CostEstimate(
            flops=2 * pieces * rows * width * blocks * feats, bytes_accessed=10 * MIB, transcendentals=0
        ),
        name="grad",
    )(raw8, gain, *res8)


def target_part(targets):
    me = {a: lax.axis_index(a) for a in AXES}
    feats = targets.shape[1] // 4
    got = []
    for t in range(4):
        pairs = []
        for source in range(256):
            rest, y = divmod(source, 4)
            rest, zh = divmod(rest, 2)
            rest, core = divmod(rest, 2)
            zl, x = divmod(rest, 4)
            column = zl ^ t
            dest = zh * 2 + y // 2
            dest = dest * 4 + (y % 2) * 2 + column // 2
            dest = dest * 2 + column % 2
            dest = dest * 2 + core
            dest = dest * 4 + x
            pairs.append((source, dest))
        part = lax.dynamic_slice_in_dim(targets, (me["zl"] ^ t) * feats, feats, 1)
        got.append(lax.ppermute(part, AXES, pairs))
    column = (me["x"] % 2) * 2 + me["core"]
    return pick(jnp.stack(got), [column ^ a for a in range(4)]).reshape(-1, feats)


def local(inputs, gate, up, down, targets, widths, gains):
    me = {a: lax.axis_index(a) for a in AXES}
    first = me["core"] == 0
    rows = inputs.shape[1]
    width = gate.shape[1]
    scale = 1.0 / rows**0.5
    contract_rows = (((0,), (0,)), ((), ()))

    mine = jnp.where(first, gate, up)
    theirs = swap(jnp.where(first, up, gate), "core")
    inputs_other = swap(inputs, "core")

    column = (me["zh"] * 4 + me["y"]) * width + lax.broadcasted_iota(jnp.int32, (1, width), 1)
    kept = (column < widths[0]).astype(jnp.float32)
    gain = gains * kept
    all_gains = gather4(gather4(gather_pair(gain[0]), "x"), "zl").reshape(32, width)
    gain8 = jnp.stack(gather_tp(all_gains))
    down8 = jnp.stack(gather_tp(down))
    target = target_part(targets)

    part = lax.dot_general(inputs, mine, contract_rows, preferred_element_type=jnp.float32)
    part = part + lax.dot_general(inputs_other, theirs, contract_rows, preferred_element_type=jnp.float32)
    part = lax.all_to_all(part.reshape(16, rows // 16, width), ("x", "y"), 0, 0, tiled=True)
    part = jnp.sum(part.reshape(4, 4, 8, 2, width), axis=0)
    part = lax.all_to_all(part.transpose(1, 0, 2, 3), ("zh", "zl"), 0, 0, tiled=True)
    part = jnp.sum(part.reshape(2, 4, 4, 2, width), axis=1)
    other = swap(part, "core")
    raw = jax.nn.silu(jnp.where(first, part, other)) * jnp.where(first, other, part)
    raw = pick(raw, [me["zh"] ^ a for a in range(2)])
    raw = pick(raw, [me["y"] ^ k for k in range(4)], 1)
    raw = gather4(gather4(raw, "zl"), "x")
    raw8 = raw.transpose(2, 3, 0, 1, 4, 5).reshape(8, rows // 8, width)

    res = output_call(raw8, gain8, down8, target)
    res_own = lax.all_to_all(res, VAR, 0, 0, tiled=True)
    res8 = gather_tp(res_own)

    raw_tp = raw8.reshape(2, 4, rows // 8, width)
    raw_own = jnp.stack([raw_tp[:, 0]] + [swap(raw_tp[:, k], "y", k) for k in (1, 2, 3)], 1)
    raw_own = jnp.concatenate([raw_own[0], swap(raw_own[1], "zh")])

    grad_down = grad_call(raw_own, gain, res8, scale)

    sums = back_call(res, raw8, down8).reshape(2, 4, 32, width)
    sums = sums[:, 0] + swap(sums[:, 1], "y", 1) + swap(sums[:, 2], "y", 2) + swap(sums[:, 3], "y", 3)
    sums = sums[0] + swap(sums[1], "zh")
    sums = jnp.sum(lax.all_to_all(sums, VAR, 0, 0, tiled=True), axis=0, keepdims=True)
    return grad_down, kept * sums * scale


def solution(mesh):
    fine = Mesh(mesh.devices.reshape(SHAPE), AXES)
    tp = ("zh", "y")
    return jax.shard_map(
        local,
        mesh=fine,
        in_specs=(P(VAR, None), P(VAR, tp), P(VAR, tp), P(tp, VAR), P(VAR, tp), P(VAR), P(VAR, tp)),
        out_specs=(P(VAR, tp, None), P(VAR, tp)),
        check_vma=False,
    )
```

```python
import functools

import jax
import jax.numpy as jnp
from jax import lax
from jax.experimental import pallas as pl
from jax.experimental.pallas import tpu as pltpu
from jax.sharding import Mesh, PartitionSpec as P

SHAPE = (4, 4, 2, 2, 4)
AXES = ("zl", "x", "core", "zh", "y")
VAR = ("zl", "x", "core")
SIZE = dict(zip(AXES, SHAPE))
MIB = 1024 * 1024
F32, BF16 = jnp.float32, jnp.bfloat16


def swap(value, axis, mask=1):
    return lax.ppermute(value, axis, [(i, i ^ mask) for i in range(SIZE[axis])])


def near4(value, axis):
    return [value] + [swap(value, axis, k) for k in (1, 2, 3)]


def after(value, other):
    return lax.optimization_barrier((value, other))[0]


def params(mib=56):
    return pltpu.CompilerParams(vmem_limit_bytes=mib * MIB)


SMEM = pl.BlockSpec(memory_space=pltpu.SMEM)
VMEM = pl.BlockSpec(memory_space=pltpu.VMEM)
HBM = pl.BlockSpec(memory_space=pl.ANY)


def part_kernel(where_ref, x_ref, x_other_ref, gate_ref, up_ref, theirs_ref, gain_ref, target_ref, out_ref):
    core = where_ref[2]
    lanes = gate_ref.shape[1] // 128
    mine = jnp.where(core == 0, gate_ref[...], up_ref[...])
    x = jnp.concatenate([x_ref[...], x_other_ref[...]]).T
    part = jnp.dot(x, jnp.concatenate([mine, theirs_ref[...]]), preferred_element_type=F32)
    target = target_ref[...].astype(F32)
    for slot in range(16):
        for e in range(2):
            for lane in range(lanes):
                at = slot * 16 + e * 8
                out_ref[slot, e * lanes + lane] = part[at : at + 8, lane * 128 : lane * 128 + 128]
        for half in range(2):
            at = ((slot // 4) % 2) * 256 + half * 128
            out_ref[slot, 2 * lanes + half] = target[:, at : at + 128]
        out_ref[slot, 2 * lanes + 2] = jnp.zeros((8, 128), F32)
        for lane in range(lanes):
            out_ref[slot, 2 * lanes + 2, lane : lane + 1, :] = gain_ref[:, lane * 128 : lane * 128 + 128]


def part_call(where, x, x_other, gate, up, theirs, gain, targets):
    lanes = gate.shape[1] // 128
    return pl.pallas_call(
        part_kernel,
        in_specs=[SMEM] + [VMEM] * 7,
        out_specs=VMEM,
        out_shape=jax.ShapeDtypeStruct((16, 2 * lanes + 3, 8, 128), F32),
        compiler_params=params(),
        name="part",
    )(where, x, x_other, gate, up, theirs, gain, targets)


def sum_kernel(where_ref, part_ref, out_ref, gain_ref, target_ref):
    lanes = out_ref.shape[1]
    for y in range(4):
        for e in range(2):
            for lane in range(lanes):
                t = e * lanes + lane
                total = (part_ref[y, t] + part_ref[4 + y, t]) + (part_ref[8 + y, t] + part_ref[12 + y, t])
                out_ref[:, lane, y * 2 + e, :] = total
    for s in range(16):
        gain_ref[s] = part_ref[s, 2 * lanes + 2]
    x, y = where_ref[0], where_ref[3]
    for high in range(2):
        for half in range(2):
            target_ref[high * 2 + half] = part_ref[y * 4 + high * 2 + x // 2, 2 * lanes + half]


def sum_call(where, part):
    lanes = (part.shape[1] - 3) // 2
    return pl.pallas_call(
        sum_kernel,
        in_specs=[SMEM, VMEM],
        out_specs=[VMEM] * 3,
        out_shape=[
            jax.ShapeDtypeStruct((8, lanes, 8, 128), F32),
            jax.ShapeDtypeStruct((16, 8, 128), F32),
            jax.ShapeDtypeStruct((4, 8, 128), F32),
        ],
        compiler_params=params(),
        name="sum_x",
    )(where, part)


def raw_kernel(where_ref, mine_ref, other_ref, out_ref):
    first = where_ref[2] == 0
    for zh in range(2):
        for lane in range(out_ref.shape[2]):
            mine = (mine_ref[zh * 4, lane] + mine_ref[zh * 4 + 1, lane]) + (mine_ref[zh * 4 + 2, lane] + mine_ref[zh * 4 + 3, lane])
            other = (other_ref[zh * 4, lane] + other_ref[zh * 4 + 1, lane]) + (other_ref[zh * 4 + 2, lane] + other_ref[zh * 4 + 3, lane])
            gate = jnp.where(first, mine, other)
            raw = jax.nn.silu(gate) * jnp.where(first, other, mine)
            for copy in range(4):
                out_ref[copy, zh, lane] = raw


def raw_call(where, mine, other):
    lanes = mine.shape[1]
    return pl.pallas_call(
        raw_kernel,
        in_specs=[SMEM, VMEM, VMEM],
        out_specs=VMEM,
        out_shape=jax.ShapeDtypeStruct((4, 2, lanes, 8, 128), F32),
        compiler_params=params(),
        name="raw",
    )(where, mine, other)


def output_kernel(where_ref, *refs):
    raw_refs, small_refs, mine_refs, theirs_refs = (refs[i : i + 4] for i in (0, 4, 8, 12))
    res_ref, own_refs = refs[16], refs[17:21]
    raw_all, small_all, down_all, hidden, total, raw_sem, small_sem, mine_sem, theirs_sem = refs[21:]
    x, zl, core, y, zh = (where_ref[i] for i in range(5))
    lanes = raw_all.shape[2]
    copies = []
    for k in range(4):
        copies.append([
            pltpu.make_async_copy(raw_refs[k], raw_all.at[pl.ds((x ^ k) * 4, 4)], raw_sem.at[k]),
            pltpu.make_async_copy(small_refs[k], small_all.at[zl ^ k], small_sem.at[k]),
            pltpu.make_async_copy(mine_refs[k], down_all.at[core, k], mine_sem.at[k]),
            pltpu.make_async_copy(theirs_refs[k], down_all.at[1 - core, k], theirs_sem.at[k]),
        ])
    for kind in range(2):
        for k in range(4):
            copies[k][kind].start()
    for k in range(4):
        copies[k][2].start()
        copies[k][3].start()
    for kind in range(2):
        for k in range(4):
            copies[k][kind].wait()
    for k in range(4):
        copies[k][2].wait()
        copies[k][3].wait()
        for a in range(2):
            unit = zh ^ a
            for e in range(2):
                for lane in range(lanes):
                    cols = slice(lane * 128, lane * 128 + 128)
                    raw = raw_all[:, unit, lane, (y ^ k) * 2 + e, :]
                    own_refs[k][a, e, :, cols] = raw
                    for v in range(16):
                        gain = small_all[v // 4, a, (v % 4) * 4 + (y ^ k), lane : lane + 1, :]
                        at = v * 32 + e * 16
                        hidden[at : at + 16, cols] = (raw * gain).astype(BF16)
            down = jnp.concatenate([down_all[0, k, a], down_all[1, k, a]], axis=1)
            term = jnp.dot(hidden[...], down, preferred_element_type=F32)
            if k == 0 and a == 0:
                total[...] = term
            else:
                total[...] += term
    source = (zl // 2) ^ zh
    for e in range(2):
        tile = 16 + 4 * jnp.where(core == e, 0, 1) + 2 * (zl % 2)
        for v in range(16):
            at = v * 32 + e * 16
            for half in range(2):
                cols = slice(half * 128, half * 128 + 128)
                target = small_all[:, source, tile + half, pl.ds(zh * 4, 4), :].reshape(16, 128)
                res_ref[v, e * 16 : e * 16 + 16, cols] = (total[at : at + 16, cols] - target).astype(BF16)


def output_call(where, raws, smalls, mine, theirs):
    lanes = raws[0].shape[2]
    width = lanes * 128
    return pl.pallas_call(
        output_kernel,
        in_specs=[SMEM] + [HBM] * 16,
        out_specs=[VMEM] * 5,
        out_shape=[jax.ShapeDtypeStruct((16, 32, 256), BF16)]
        + [jax.ShapeDtypeStruct((2, 2, 16, width), F32)] * 4,
        scratch_shapes=[
            pltpu.VMEM((16, 2, lanes, 8, 128), F32),
            pltpu.VMEM((4,) + smalls[0].shape, F32),
            pltpu.VMEM((2, 4) + mine[0].shape, BF16),
            pltpu.VMEM((512, width), BF16),
            pltpu.VMEM((512, 256), F32),
        ]
        + [pltpu.SemaphoreType.DMA((4,))] * 4,
        compiler_params=params(),
        cost_estimate=pl.CostEstimate(flops=2 * 512 * 8 * width * 256, bytes_accessed=6 * MIB, transcendentals=0),
        name="output",
    )(where, *raws, *smalls, *mine, *theirs)


def back_kernel(where_ref, *refs):
    res_ref, own_refs, mine_refs, theirs_refs, out_refs = refs[0], refs[1:5], refs[5:9], refs[9:13], refs[13:]
    first = where_ref[2] == 0
    for k in range(4):
        for a in range(2):
            mine, theirs = mine_refs[k][a], theirs_refs[k][a]
            down = jnp.concatenate([jnp.where(first, mine, theirs), jnp.where(first, theirs, mine)], axis=1)
            raw = jnp.concatenate([own_refs[k][a, 0], own_refs[k][a, 1]])
            for at in range(0, 16, 8):
                res = res_ref[at : at + 8].reshape(256, 256)
                back = lax.dot_general(res, down, (((1,), (1,)), ((), ())), preferred_element_type=F32)
                out_refs[k][a, at : at + 8, :] = jnp.sum(back.reshape(8, 32, -1) * raw[None], axis=1)


def back_call(where, res, owns, mine, theirs):
    width = owns[0].shape[3]
    return pl.pallas_call(
        back_kernel,
        in_specs=[SMEM] + [VMEM] * 13,
        out_specs=[VMEM] * 4,
        out_shape=[jax.ShapeDtypeStruct((2, 16, width), F32)] * 4,
        compiler_params=params(),
        cost_estimate=pl.CostEstimate(flops=2 * 512 * 8 * width * 256, bytes_accessed=6 * MIB, transcendentals=0),
        name="back",
    )(where, res, *owns, *mine, *theirs)


def pick_kernel(where_ref, *refs):
    for k in range(4):
        refs[4][k] = refs[k][1, where_ref[2]]


def pick_call(where, owns):
    shape = owns[0].shape
    return pl.pallas_call(
        pick_kernel,
        in_specs=[SMEM] + [VMEM] * 4,
        out_specs=VMEM,
        out_shape=jax.ShapeDtypeStruct((4,) + shape[2:], F32),
        compiler_params=params(),
        name="pick",
    )(where, *owns)


def grad_kernel(scale, where_ref, gain_ref, *refs):
    own_refs, far_ref, far_other_ref, res_refs = refs[:4], refs[4], refs[5], refs[6:14]
    out_ref, hidden_t, block = refs[14:]
    core = where_ref[2]
    some, rows, feats = res_refs[0].shape
    width = gain_ref.shape[1]

    @pl.when(pl.program_id(0) == 0)
    def _():
        for k in range(4):
            for e in range(2):
                far = jnp.where(core == e, far_ref[k], far_other_ref[k])
                for a, raw in enumerate((own_refs[k][0, e], far)):
                    at = (a * 4 + k) * rows + e * 16
                    block[at : at + 16, :width] = (raw * gain_ref[...]).astype(BF16)
        hidden_t[...] = block[:, :width].T

    for p in range(8):
        for q in range(some):
            block[p * rows : (p + 1) * rows, q * feats : (q + 1) * feats] = res_refs[p][q]
    grad = jnp.dot(hidden_t[...], block[:, : some * feats], preferred_element_type=F32)
    out_ref[0] = (grad * scale).astype(BF16)


def grad_call(where, gain, owns, far, far_other, res8, scale):
    width = gain.shape[1]
    blocks, rows, feats = res8[0].shape
    some = 2
    whole = lambda shape: pl.BlockSpec(shape, lambda s, w: (0,) * len(shape))
    return pl.pallas_call(
        functools.partial(grad_kernel, scale),
        grid_spec=pltpu.PrefetchScalarGridSpec(
            num_scalar_prefetch=1,
            grid=(blocks // some,),
            in_specs=[whole(gain.shape)]
            + [pl.BlockSpec((1,) + owns[0].shape[1:], lambda s, w: (0, 0, 0, 0))] * 4
            + [whole(far.shape)] * 2
            + [pl.BlockSpec((some, rows, feats), lambda s, w: (s, 0, 0))] * 8,
            out_specs=pl.BlockSpec((1, width, some * feats), lambda s, w: (0, 0, s)),
            scratch_shapes=[
                pltpu.VMEM((width, 8 * rows), BF16),
                pltpu.VMEM((8 * rows, max(width, some * feats)), BF16),
            ],
        ),
        out_shape=jax.ShapeDtypeStruct((1, width, blocks * feats), BF16),
        compiler_params=params(),
        cost_estimate=pl.CostEstimate(
            flops=2 * 8 * rows * width * blocks * feats, bytes_accessed=10 * MIB, transcendentals=0
        ),
        name="grad",
    )(where, gain, *owns, far, far_other, *res8)


def local(inputs, gate, up, down, targets, widths, gains):
    me = {a: lax.axis_index(a) for a in AXES}
    where = jnp.stack([me["x"], me["zl"], me["core"], me["y"], me["zh"]]).astype(jnp.int32)
    first = me["core"] == 0
    rows = inputs.shape[1]
    width = gate.shape[1]
    scale = 1.0 / rows**0.5

    column = (me["zh"] * 4 + me["y"]) * width + lax.broadcasted_iota(jnp.int32, (1, width), 1)
    kept = (column < widths[0]).astype(F32)
    gain = gains * kept

    theirs = swap(jnp.where(first, up, gate), "core")
    inputs_other = swap(inputs, "core")
    part = part_call(where, inputs, inputs_other, gate, up, theirs, gain, targets)
    down_pair = after(down, part)
    part = lax.all_to_all(part, ("x", "y"), 0, 0, tiled=True)
    part, gain_xy, target_xy = sum_call(where, part)
    part = lax.all_to_all(part, ("zh", "zl"), 0, 0, tiled=True)
    raw = raw_call(where, part, swap(part, "core"))
    raws = near4(lax.all_to_all(raw, "zl", 0, 0, tiled=True), "x")

    small = jnp.concatenate([gain_xy, target_xy, swap(target_xy, "core")])
    smalls = near4(jnp.stack([small, swap(small, "zh")]), "zl")

    down_pair = jnp.stack([down_pair, swap(down_pair, "zh")])
    mine = near4(down_pair, "y")
    theirs = [swap(d, "core") for d in mine]

    res, *owns = output_call(where, raws, smalls, mine, theirs)
    res_own = lax.all_to_all(res, ("zl", "x"), 0, 0, tiled=True)
    res8 = near4(res_own, "y") + near4(swap(res_own, "zh"), "y")

    got = [owns[0]] + [swap(owns[k], "y", k) for k in (1, 2, 3)]
    far = swap(pick_call(where, got), "zh")
    grad_down = grad_call(where, gain, got, far, swap(far, "core"), res8, scale)

    sums = back_call(where, after(res, res_own), owns, mine, theirs)
    sums = sums[0] + swap(sums[1], "y", 1) + swap(sums[2], "y", 2) + swap(sums[3], "y", 3)
    sums = sums[0] + swap(sums[1], "zh")
    sums = jnp.sum(lax.all_to_all(sums, ("zl", "x"), 0, 0, tiled=True), axis=0, keepdims=True)
    return grad_down, kept * sums * scale


def solution(mesh):
    fine = Mesh(mesh.devices.reshape(SHAPE), AXES)
    tp = ("zh", "y")
    return jax.shard_map(
        local,
        mesh=fine,
        in_specs=(P(VAR, None), P(VAR, tp), P(VAR, tp), P(tp, VAR), P(VAR, tp), P(VAR), P(VAR, tp)),
        out_specs=(P(VAR, tp, None), P(VAR, tp)),
        check_vma=False,
    )
```

```python
import functools

import jax
import jax.numpy as jnp
from jax import lax
from jax.experimental import pallas as pl
from jax.experimental.pallas import tpu as pltpu
from jax.sharding import Mesh, PartitionSpec as P

SHAPE = (4, 4, 2, 2, 4)
AXES = ("zl", "x", "core", "zh", "y")
VAR = ("zl", "x", "core")
SIZE = dict(zip(AXES, SHAPE))
MIB = 1024 * 1024
F32, BF16 = jnp.float32, jnp.bfloat16


def swap(value, axis, mask=1):
    if mask == 0:
        return value
    return lax.ppermute(value, axis, [(i, i ^ mask) for i in range(SIZE[axis])])


def near4(value, axis):
    return [value] + [swap(value, axis, k) for k in (1, 2, 3)]


def after(value, other):
    return lax.optimization_barrier((value, other))[0]


def params(mib=56):
    return pltpu.CompilerParams(vmem_limit_bytes=mib * MIB)


SMEM = pl.BlockSpec(memory_space=pltpu.SMEM)
VMEM = pl.BlockSpec(memory_space=pltpu.VMEM)
HBM = pl.BlockSpec(memory_space=pl.ANY)


def part_kernel(x_ref, x_other_ref, gate_ref, up_ref, theirs_ref, width_ref, gains_ref, target_ref, out_ref, gain_ref):
    core = lax.axis_index("core")
    lanes = gate_ref.shape[1] // 128
    mine = jnp.where(core == 0, gate_ref[...], up_ref[...])
    x = jnp.concatenate([x_ref[...], x_other_ref[...]]).T
    part = jnp.dot(x, jnp.concatenate([mine, theirs_ref[...]]), preferred_element_type=F32)
    target = target_ref[...].astype(F32)
    width = gate_ref.shape[1]
    column = (lax.axis_index("zh") * 4 + lax.axis_index("y")) * width + lax.broadcasted_iota(jnp.int32, (1, width), 1)
    gain = jnp.where(column < width_ref[0], gains_ref[...], 0.0)
    gain_ref[...] = gain
    for slot in range(16):
        for e in range(2):
            for lane in range(lanes):
                at = slot * 16 + e * 8
                out_ref[slot, e * lanes + lane] = part[at : at + 8, lane * 128 : lane * 128 + 128]
        for half in range(2):
            at = ((slot // 4) % 2) * 256 + half * 128
            out_ref[slot, 2 * lanes + half] = target[:, at : at + 128]
        out_ref[slot, 2 * lanes + 2] = jnp.zeros((8, 128), F32)
        for lane in range(lanes):
            out_ref[slot, 2 * lanes + 2, lane : lane + 1, :] = gain[:, lane * 128 : lane * 128 + 128]


def part_call(x, x_other, gate, up, theirs, widths, gains, targets):
    lanes = gate.shape[1] // 128
    return pl.pallas_call(
        part_kernel,
        in_specs=[VMEM] * 5 + [SMEM] + [VMEM] * 2,
        out_specs=[VMEM] * 2,
        out_shape=[
            jax.ShapeDtypeStruct((16, 2 * lanes + 3, 8, 128), F32),
            jax.ShapeDtypeStruct(gains.shape, F32),
        ],
        compiler_params=params(),
        name="part",
    )(x, x_other, gate, up, theirs, widths, gains, targets)


def sum_kernel(part_ref, out_ref):
    lanes = out_ref.shape[1] - 6
    for y in range(4):
        for e in range(2):
            for lane in range(lanes):
                t = e * lanes + lane
                total = (part_ref[y, t] + part_ref[4 + y, t]) + (part_ref[8 + y, t] + part_ref[12 + y, t])
                out_ref[:, lane, y * 2 + e, :] = total
    x, y = lax.axis_index("x"), lax.axis_index("y")
    for high in range(2):
        for half in range(2):
            target = part_ref[y * 4 + high * 2 + x // 2, 2 * lanes + half]
            for slot in range(high, 8, 2):
                out_ref[slot, lanes + half] = target
    for k in range(4):
        gain = part_ref[x * 4 + k, 2 * lanes + 2]
        for slot in range(8):
            out_ref[slot, lanes + 2 + k] = gain


def sum_call(part):
    lanes = (part.shape[1] - 3) // 2
    return pl.pallas_call(
        sum_kernel,
        in_specs=[VMEM],
        out_specs=VMEM,
        out_shape=jax.ShapeDtypeStruct((8, lanes + 6, 8, 128), F32),
        compiler_params=params(),
        name="sum_x",
    )(part)


def raw_kernel(mine_ref, other_ref, out_ref, target_ref, gain_ref):
    first = lax.axis_index("core") == 0
    lanes = out_ref.shape[1]
    unit = lax.axis_index("core") * 4
    for lane in range(lanes):
        mine, other = (
            (r[unit, lane] + r[unit + 1, lane]) + (r[unit + 2, lane] + r[unit + 3, lane]) for r in (mine_ref, other_ref)
        )
        raw = jax.nn.silu(jnp.where(first, mine, other)) * jnp.where(first, other, mine)
        for copy in range(4):
            out_ref[copy, lane] = raw
    gain_ref[...] = mine_ref[:, lanes + 2 :]
    source, row = (lax.axis_index("zl") // 2) * 4, lax.axis_index("zh")
    for half in range(2):
        cols = slice(half * 128, half * 128 + 128)
        for x in range(4):
            own, far = mine_ref[source + x, lanes + half], other_ref[source + x, lanes + half]
            for e in range(2):
                target = jnp.where(first == (e == 0), own, far)
                target_ref[e, x * 4 : x * 4 + 4, cols] = jnp.where(row == 0, target[:4], target[4:])


def raw_call(mine, other):
    lanes = mine.shape[1] - 6
    return pl.pallas_call(
        raw_kernel,
        in_specs=[VMEM, VMEM],
        out_specs=[VMEM] * 3,
        out_shape=[
            jax.ShapeDtypeStruct((4, lanes, 8, 128), F32),
            jax.ShapeDtypeStruct((2, 16, 256), F32),
            jax.ShapeDtypeStruct((8, 4, 8, 128), F32),
        ],
        compiler_params=params(),
        name="raw",
    )(mine, other)


def extract_kernel(*refs):
    x, core, y, zh = (lax.axis_index(a) for a in ("x", "core", "y", "zh"))
    raw_refs, other_refs, out_refs, both = refs[:4], refs[4:8], refs[8:10], refs[10]
    for k in range(4):
        at = pl.ds((x ^ k) * 4, 4)
        both[core, at] = raw_refs[k][...]
        both[1 - core, at] = other_refs[k][...]
    for a in range(2):
        for k in range(4):
            for lane in range(both.shape[2]):
                out_refs[a][k, :, lane * 128 : lane * 128 + 128] = both[zh ^ a, :, lane, (y ^ k) * 2 + core, :]


def extract_call(raws, others):
    lanes = raws[0].shape[1]
    return pl.pallas_call(
        extract_kernel,
        in_specs=[VMEM] * 8,
        out_specs=[VMEM] * 2,
        out_shape=[jax.ShapeDtypeStruct((4, 16, lanes * 128), F32)] * 2,
        scratch_shapes=[pltpu.VMEM((2, 16, lanes, 8, 128), F32)],
        compiler_params=params(),
        name="extract",
    )(*raws, *others)


def output_kernel(*refs):
    raw_refs, other_refs, gain_refs, mine_refs, theirs_refs = refs[:4], refs[4:8], refs[8:12], refs[12:20], refs[20:28]
    target_ref, res_ref, row_refs = refs[28], refs[29], refs[30:34]
    raw_all, gain_all, down_all, hidden, total, raw_sem, gain_sem, mine_sem, theirs_sem = refs[34:]
    x, core, y, zh = (lax.axis_index(a) for a in ("x", "core", "y", "zh"))
    lanes = raw_all.shape[2]
    first, second = [], []
    for k in range(4):
        at = pl.ds((x ^ k) * 4, 4)
        first.append(pltpu.make_async_copy(raw_refs[k], raw_all.at[core, at], raw_sem.at[k]))
        first.append(pltpu.make_async_copy(other_refs[k], raw_all.at[1 - core, at], raw_sem.at[4 + k]))
        first.append(pltpu.make_async_copy(gain_refs[k], gain_all.at[x ^ k], gain_sem.at[k]))
    for p in range(8):
        second.append(pltpu.make_async_copy(mine_refs[p], down_all.at[core, p], mine_sem.at[p]))
        second.append(pltpu.make_async_copy(theirs_refs[p], down_all.at[1 - core, p], theirs_sem.at[p]))
    for copy in first + second:
        copy.start()
    for copy in first:
        copy.wait()
    for p in range(8):
        second[2 * p].wait()
        second[2 * p + 1].wait()
        a, k = p // 4, p % 4
        unit, other = zh ^ a, y ^ k
        for lane in range(lanes):
            cols = slice(lane * 128, lane * 128 + 128)
            for e in range(2):
                raw = raw_all[unit, :, lane, other * 2 + e, :]
                row_refs[k][a, e, :, cols] = raw
                for v in range(16):
                    gain = gain_all[v % 4, unit * 4 + v // 4, other, lane : lane + 1, :]
                    at = v * 32 + e * 16
                    hidden[at : at + 16, cols] = (raw * gain).astype(BF16)
        down = jnp.concatenate([down_all[0, p], down_all[1, p]], axis=1)
        term = jnp.dot(hidden[...], down, preferred_element_type=F32)
        if p == 0:
            total[...] = term
        else:
            total[...] += term
    for e in range(2):
        target = target_ref[e]
        for v in range(16):
            at = v * 32 + e * 16
            res = (total[at : at + 16, :] - target).astype(BF16)
            for copy in range(2):
                res_ref[copy * 16 + v, e * 16 : e * 16 + 16, :] = res


def output_call(raws, others, gains, mine, theirs, target):
    lanes = raws[0].shape[1]
    width = lanes * 128
    return pl.pallas_call(
        output_kernel,
        in_specs=[HBM] * 28 + [VMEM],
        out_specs=[VMEM] * 5,
        out_shape=[jax.ShapeDtypeStruct((32, 32, 256), BF16)]
        + [jax.ShapeDtypeStruct((2, 2, 16, width), F32)] * 4,
        scratch_shapes=[
            pltpu.VMEM((2, 16, lanes, 8, 128), F32),
            pltpu.VMEM((4,) + gains[0].shape, F32),
            pltpu.VMEM((2, 8) + mine[0].shape, BF16),
            pltpu.VMEM((512, width), BF16),
            pltpu.VMEM((512, 256), F32),
            pltpu.SemaphoreType.DMA((8,)),
            pltpu.SemaphoreType.DMA((4,)),
            pltpu.SemaphoreType.DMA((8,)),
            pltpu.SemaphoreType.DMA((8,)),
        ],
        compiler_params=params(),
        cost_estimate=pl.CostEstimate(flops=2 * 512 * 8 * width * 256, bytes_accessed=6 * MIB, transcendentals=0),
        name="output",
    )(*raws, *others, *gains, *mine, *theirs, target)


def back_kernel(*refs):
    res_ref, own_refs, mine_refs, theirs_refs, out_ref = refs[0], refs[1:5], refs[5:13], refs[13:21], refs[21]
    first = lax.axis_index("core") == 0
    for k in range(4):
        for a in range(2):
            mine, theirs = mine_refs[a * 4 + k][...], theirs_refs[a * 4 + k][...]
            down = jnp.concatenate([jnp.where(first, mine, theirs), jnp.where(first, theirs, mine)], axis=1)
            raw = jnp.concatenate([own_refs[k][a, 0], own_refs[k][a, 1]])
            for at in range(0, 16, 8):
                res = res_ref[at : at + 8].reshape(256, 256)
                back = lax.dot_general(res, down, (((1,), (1,)), ((), ())), preferred_element_type=F32)
                out_ref[at : at + 8, a * 4 + k, :] = jnp.sum(back.reshape(8, 32, -1) * raw[None], axis=1)


def back_call(res, owns, mine, theirs):
    width = owns[0].shape[3]
    return pl.pallas_call(
        back_kernel,
        in_specs=[VMEM] * 21,
        out_specs=VMEM,
        out_shape=jax.ShapeDtypeStruct((16, 8, width), F32),
        compiler_params=params(),
        cost_estimate=pl.CostEstimate(flops=2 * 512 * 8 * width * 256, bytes_accessed=6 * MIB, transcendentals=0),
        name="back",
    )(res, *owns, *mine, *theirs)


def total_kernel(part_ref, out_ref):
    y, zh = lax.axis_index("y"), lax.axis_index("zh")
    total = jnp.sum(part_ref[...], axis=0)
    for a in range(2):
        for k in range(4):
            p = a * 4 + k
            at = (zh ^ a) * 4 + (y ^ k)
            out_ref[at] = jnp.zeros((8, 128), F32)
            for lane in range(total.shape[1] // 128):
                out_ref[at, lane : lane + 1, :] = total[p : p + 1, lane * 128 : lane * 128 + 128]


def total_call(part):
    return pl.pallas_call(
        total_kernel,
        in_specs=[VMEM],
        out_specs=VMEM,
        out_shape=jax.ShapeDtypeStruct((8, 8, 128), F32),
        compiler_params=params(),
        name="total",
    )(part)


def pair_kernel(near_ref, far_ref, *out_refs):
    for k in range(4):
        out_refs[k][0] = near_ref[k]
        out_refs[k][1] = far_ref[k]


def pair_call(near, far):
    return pl.pallas_call(
        pair_kernel,
        in_specs=[VMEM] * 2,
        out_specs=[VMEM] * 4,
        out_shape=[jax.ShapeDtypeStruct((2,) + near.shape[1:], F32)] * 4,
        compiler_params=params(),
        name="pair",
    )(near, far)


def hidden_kernel(gain_ref, *refs):
    mine_refs, other_refs, out_ref, block = refs[:4], refs[4:8], refs[8], refs[9]
    core, zh = lax.axis_index("core"), lax.axis_index("zh")
    gain = gain_ref[...]
    for k in range(4):
        for z in range(2):
            for e in range(2):
                raw = jnp.where(core == e, mine_refs[k][zh ^ z], other_refs[k][zh ^ z])
                at = (k * 2 + z) * 32 + e * 16
                block[at : at + 16, :] = (raw * gain).astype(BF16)
    out_ref[...] = block[...].T


def hidden_call(gain, mine, others):
    width = gain.shape[1]
    return pl.pallas_call(
        hidden_kernel,
        in_specs=[VMEM] * 9,
        out_specs=VMEM,
        out_shape=jax.ShapeDtypeStruct((width, 256), BF16),
        scratch_shapes=[pltpu.VMEM((256, width), BF16)],
        compiler_params=params(),
        name="hidden",
    )(gain, *mine, *others)


def grad_kernel(scale, hidden_ref, *refs):
    res_refs, out_ref, res_all, sem = refs[:4], refs[4], refs[5], refs[6]
    step = pl.program_id(0)

    @pl.when(step == 0)
    def _():
        copies = [pltpu.make_async_copy(res_refs[k], res_all.at[k], sem.at[k]) for k in range(4)]
        for c in copies:
            c.start()
        for c in copies:
            c.wait()

    some = out_ref.shape[2] // 256
    block = jnp.concatenate(
        [
            jnp.concatenate([res_all[k, z * 16 + step * some + q] for k in range(4) for z in range(2)])
            for q in range(some)
        ],
        axis=1,
    )
    grad = jnp.dot(hidden_ref[...], block, preferred_element_type=F32)
    out_ref[0] = (grad * scale).astype(BF16)


def grad_call(hidden, res4, scale):
    width = hidden.shape[0]
    pieces, rows, feats = res4[0].shape
    blocks, some = pieces // 2, 2
    return pl.pallas_call(
        functools.partial(grad_kernel, scale),
        grid=(blocks // some,),
        in_specs=[pl.BlockSpec(hidden.shape, lambda s: (0, 0))] + [HBM] * 4,
        out_specs=pl.BlockSpec((1, width, some * feats), lambda s: (0, 0, s)),
        out_shape=jax.ShapeDtypeStruct((1, width, blocks * feats), BF16),
        scratch_shapes=[pltpu.VMEM((4, pieces, rows, feats), BF16), pltpu.SemaphoreType.DMA((4,))],
        compiler_params=params(),
        cost_estimate=pl.CostEstimate(
            flops=40 * 8 * rows * width * blocks * feats, bytes_accessed=10 * MIB, transcendentals=0
        ),
        name="grad",
    )(hidden, *res4)


def local(inputs, gate, up, down, targets, widths, gains):
    me = {a: lax.axis_index(a) for a in AXES}
    first = me["core"] == 0
    rows = inputs.shape[1]
    width = gate.shape[1]
    scale = 1.0 / rows**0.5

    theirs = swap(jnp.where(first, up, gate), "core")
    inputs_other = swap(inputs, "core")
    part, gain = part_call(inputs, inputs_other, gate, up, theirs, widths, gains, targets)
    down = after(down, part)
    part = lax.all_to_all(part, ("x", "y"), 0, 0, tiled=True)
    far = swap(down, "zh")
    part = sum_call(after(part, far))
    down, far = after((down, far), part)
    part = lax.all_to_all(part, ("zh", "zl"), 0, 0, tiled=True)
    mine = near4(down, "y")
    part = after(part, mine)
    raw, target, gain_z = raw_call(part, swap(part, "core"))
    mine = after(mine, raw)
    raw = lax.all_to_all(raw, "zl", 0, 0, tiled=True)
    theirs = [swap(d, "core") for d in mine]
    raw = after(raw, theirs)
    raws = near4(raw, "x")
    others = [swap(r, "core") for r in raws]
    far, gain_z = after((far, gain_z), raw)
    mine_far = near4(far, "y")
    theirs_far = [swap(d, "core") for d in mine_far]
    all_gains = near4(gain_z, "x")
    mine, theirs = mine + mine_far, theirs + theirs_far

    near, far = extract_call(raws, others)
    far = swap(far, "zh")
    raws, others = after((raws, others), near)

    res, *rows8 = output_call(raws, others, all_gains, mine, theirs, target)
    res_own = lax.all_to_all(after(res, far), ("zh", "zl", "x"), 0, 0, tiled=True)
    owns = pair_call(*after((near, far), res))
    got = [owns[0]] + [swap(owns[k], "y", k) for k in (1, 2, 3)]
    sums = back_call(after(res, owns), rows8, mine, theirs)
    res_own = after(res_own, (sums, got))
    res4 = near4(res_own, "y")
    sums, got = after((sums, got), res_own)
    sums = lax.all_to_all(sums, ("zl", "x"), 0, 0, tiled=True)
    hidden = hidden_call(gain, got, [swap(g, "core") for g in got])
    sums = lax.all_to_all(total_call(sums), ("zh", "y"), 0, 0, tiled=True)
    grad_down = grad_call(hidden, res4, scale)
    sums = jnp.sum(after(sums, grad_down), axis=0)[: width // 128].reshape(1, width)
    column = (me["zh"] * 4 + me["y"]) * width + lax.broadcasted_iota(jnp.int32, (1, width), 1)
    kept = (column < widths[0]).astype(F32)
    return grad_down, kept * sums * scale


def solution(mesh):
    fine = Mesh(mesh.devices.reshape(SHAPE), AXES)
    tp = ("zh", "y")
    return jax.shard_map(
        local,
        mesh=fine,
        in_specs=(P(VAR, None), P(VAR, tp), P(VAR, tp), P(tp, VAR), P(VAR, tp), P(VAR), P(VAR, tp)),
        out_specs=(P(VAR, tp, None), P(VAR, tp)),
        check_vma=False,
    )
```

```python
import functools

import jax
import jax.numpy as jnp
from jax import lax
from jax.experimental import pallas as pl
from jax.experimental.pallas import tpu as pltpu
from jax.sharding import Mesh, PartitionSpec as P

SHAPE = (4, 4, 2, 2, 4)
AXES = ("zl", "x", "core", "zh", "y")
VAR = ("zl", "x", "core")
SIZE = dict(zip(AXES, SHAPE))
MIB = 1024 * 1024
F32, BF16 = jnp.float32, jnp.bfloat16


def swap(value, axis, mask=1):
    if mask == 0:
        return value
    return lax.ppermute(value, axis, [(i, i ^ mask) for i in range(SIZE[axis])])


def near4(value, axis):
    return [value] + [swap(value, axis, k) for k in (1, 2, 3)]


def after(value, other):
    return lax.optimization_barrier((value, other))[0]


def params(mib=56):
    return pltpu.CompilerParams(vmem_limit_bytes=mib * MIB)


SMEM = pl.BlockSpec(memory_space=pltpu.SMEM)
VMEM = pl.BlockSpec(memory_space=pltpu.VMEM)
HBM = pl.BlockSpec(memory_space=pltpu.HBM)


def part_kernel(x_ref, x_other_ref, gate_ref, up_ref, theirs_ref, width_ref, gains_ref, target_ref, out_ref, gain_ref):
    core = lax.axis_index("core")
    lanes = gate_ref.shape[1] // 128
    mine = jnp.where(core == 0, gate_ref[...], up_ref[...])
    x = jnp.concatenate([x_ref[...], x_other_ref[...]]).T
    part = jnp.dot(x, jnp.concatenate([mine, theirs_ref[...]]), preferred_element_type=F32)
    target = target_ref[...].astype(F32)
    width = gate_ref.shape[1]
    column = (lax.axis_index("zh") * 4 + lax.axis_index("y")) * width + lax.broadcasted_iota(jnp.int32, (1, width), 1)
    gain = jnp.where(column < width_ref[0], gains_ref[...], 0.0)
    gain_ref[...] = gain
    for slot in range(16):
        for e in range(2):
            for lane in range(lanes):
                at = slot * 16 + e * 8
                out_ref[slot, e * lanes + lane] = part[at : at + 8, lane * 128 : lane * 128 + 128]
        for half in range(2):
            at = ((slot // 4) % 2) * 256 + half * 128
            out_ref[slot, 2 * lanes + half] = target[:, at : at + 128]
        out_ref[slot, 2 * lanes + 2] = jnp.zeros((8, 128), F32)
        for lane in range(lanes):
            out_ref[slot, 2 * lanes + 2, lane : lane + 1, :] = gain[:, lane * 128 : lane * 128 + 128]


def part_call(x, x_other, gate, up, theirs, widths, gains, targets):
    lanes = gate.shape[1] // 128
    return pl.pallas_call(
        part_kernel,
        in_specs=[VMEM] * 5 + [SMEM] + [VMEM] * 2,
        out_specs=[VMEM] * 2,
        out_shape=[
            jax.ShapeDtypeStruct((16, 2 * lanes + 3, 8, 128), F32),
            jax.ShapeDtypeStruct(gains.shape, F32),
        ],
        compiler_params=params(),
        name="part",
    )(x, x_other, gate, up, theirs, widths, gains, targets)


def sum_kernel(part_ref, out_ref, held, sem):
    lanes = out_ref.shape[1] - 6
    copies = [
        pltpu.make_async_copy(part_ref.at[i * 4 + y], held.at[i * 4 + y], sem.at[i * 4 + y])
        for y in range(4)
        for i in range(4)
    ]
    for copy in copies:
        copy.start()
    for y in range(4):
        for copy in copies[y * 4 : y * 4 + 4]:
            copy.wait()
        for e in range(2):
            for lane in range(lanes):
                t = e * lanes + lane
                total = (held[y, t] + held[4 + y, t]) + (held[8 + y, t] + held[12 + y, t])
                out_ref[:, lane, y * 2 + e, :] = total
    x, y = lax.axis_index("x"), lax.axis_index("y")
    for high in range(2):
        for half in range(2):
            target = held[y * 4 + high * 2 + x // 2, 2 * lanes + half]
            for slot in range(high, 8, 2):
                out_ref[slot, lanes + half] = target
    for k in range(4):
        gain = held[k * 4 + y, 2 * lanes + 2]
        for slot in range(8):
            out_ref[slot, lanes + 2 + k] = gain


def sum_call(part):
    lanes = (part.shape[1] - 3) // 2
    return pl.pallas_call(
        sum_kernel,
        in_specs=[HBM],
        out_specs=VMEM,
        out_shape=jax.ShapeDtypeStruct((8, lanes + 6, 8, 128), F32),
        scratch_shapes=[pltpu.VMEM(part.shape, F32), pltpu.SemaphoreType.DMA((16,))],
        compiler_params=params(),
        name="sum_x",
    )(part)


def raw_kernel(mine_ref, other_ref, out_ref, target_ref, gain_ref):
    first = lax.axis_index("core") == 0
    lanes = out_ref.shape[1]
    unit = lax.axis_index("core") * 4
    for lane in range(lanes):
        mine, other = (
            (r[unit, lane] + r[unit + 1, lane]) + (r[unit + 2, lane] + r[unit + 3, lane]) for r in (mine_ref, other_ref)
        )
        raw = jax.nn.silu(jnp.where(first, mine, other)) * jnp.where(first, other, mine)
        for copy in range(4):
            out_ref[copy, lane] = raw
    gain_ref[...] = mine_ref[:, lanes + 2 :]
    source, row = (lax.axis_index("zl") // 2) * 4, lax.axis_index("zh")
    for half in range(2):
        cols = slice(half * 128, half * 128 + 128)
        for x in range(4):
            own, far = mine_ref[source + x, lanes + half], other_ref[source + x, lanes + half]
            for e in range(2):
                target = jnp.where(first == (e == 0), own, far)
                target_ref[e, x * 4 : x * 4 + 4, cols] = jnp.where(row == 0, target[:4], target[4:])


def raw_call(mine, other):
    lanes = mine.shape[1] - 6
    return pl.pallas_call(
        raw_kernel,
        in_specs=[VMEM, VMEM],
        out_specs=[VMEM] * 3,
        out_shape=[
            jax.ShapeDtypeStruct((4, lanes, 8, 128), F32),
            jax.ShapeDtypeStruct((2, 16, 256), F32),
            jax.ShapeDtypeStruct((8, 4, 8, 128), F32),
        ],
        compiler_params=params(),
        name="raw",
    )(mine, other)


def extract_kernel(*refs):
    x, core, y, zh = (lax.axis_index(a) for a in ("x", "core", "y", "zh"))
    raw_refs, other_refs, out_refs, both = refs[:4], refs[4:8], refs[8:10], refs[10]
    for k in range(4):
        at = pl.ds((x ^ k) * 4, 4)
        both[core, at] = raw_refs[k][...]
        both[1 - core, at] = other_refs[k][...]
    for a in range(2):
        for k in range(4):
            for lane in range(both.shape[2]):
                out_refs[a][k, :, lane * 128 : lane * 128 + 128] = both[zh ^ a, :, lane, (y ^ k) * 2 + core, :]


def extract_call(raws, others):
    lanes = raws[0].shape[1]
    return pl.pallas_call(
        extract_kernel,
        in_specs=[VMEM] * 8,
        out_specs=[VMEM] * 2,
        out_shape=[jax.ShapeDtypeStruct((4, 16, lanes * 128), F32)] * 2,
        scratch_shapes=[pltpu.VMEM((2, 16, lanes, 8, 128), F32)],
        compiler_params=params(),
        name="extract",
    )(*raws, *others)


def output_kernel(*refs):
    raw_refs, other_refs, gain_refs, mine_refs, theirs_refs = refs[:4], refs[4:8], refs[8:12], refs[12:20], refs[20:28]
    target_ref, res_ref, row_refs = refs[28], refs[29], refs[30:34]
    raw_all, gain_all, down_all, hidden, total, raw_sem, gain_sem, mine_sem, theirs_sem = refs[34:]
    x, core, y, zh = (lax.axis_index(a) for a in ("x", "core", "y", "zh"))
    lanes = raw_all.shape[2]
    first, second = [], []
    for k in range(4):
        at = pl.ds((x ^ k) * 4, 4)
        first.append(pltpu.make_async_copy(raw_refs[k], raw_all.at[core, at], raw_sem.at[k]))
        first.append(pltpu.make_async_copy(other_refs[k], raw_all.at[1 - core, at], raw_sem.at[4 + k]))
        first.append(pltpu.make_async_copy(gain_refs[k], gain_all.at[y ^ k], gain_sem.at[k]))
    for p in range(8):
        second.append(pltpu.make_async_copy(mine_refs[p], down_all.at[core, p], mine_sem.at[p]))
        second.append(pltpu.make_async_copy(theirs_refs[p], down_all.at[1 - core, p], theirs_sem.at[p]))
    for copy in first + second:
        copy.start()
    for copy in first:
        copy.wait()
    for p in range(8):
        second[2 * p].wait()
        second[2 * p + 1].wait()
        a, k = p // 4, p % 4
        unit, other = zh ^ a, y ^ k
        for lane in range(lanes):
            cols = slice(lane * 128, lane * 128 + 128)
            for e in range(2):
                raw = raw_all[unit, :, lane, other * 2 + e, :]
                row_refs[k][a, e, :, cols] = raw
                for v in range(16):
                    gain = gain_all[other, unit * 4 + v // 4, v % 4, lane : lane + 1, :]
                    at = v * 32 + e * 16
                    hidden[at : at + 16, cols] = (raw * gain).astype(BF16)
        down = jnp.concatenate([down_all[0, p], down_all[1, p]], axis=1)
        term = jnp.dot(hidden[...], down, preferred_element_type=F32)
        if p == 0:
            total[...] = term
        else:
            total[...] += term
    for e in range(2):
        target = target_ref[e]
        for v in range(16):
            at = v * 32 + e * 16
            res = (total[at : at + 16, :] - target).astype(BF16)
            for copy in range(2):
                res_ref[copy * 16 + v, e * 16 : e * 16 + 16, :] = res


def output_call(raws, others, gains, mine, theirs, target):
    lanes = raws[0].shape[1]
    width = lanes * 128
    return pl.pallas_call(
        output_kernel,
        in_specs=[HBM] * 28 + [VMEM],
        out_specs=[VMEM] * 5,
        out_shape=[jax.ShapeDtypeStruct((32, 32, 256), BF16)]
        + [jax.ShapeDtypeStruct((2, 2, 16, width), F32)] * 4,
        scratch_shapes=[
            pltpu.VMEM((2, 16, lanes, 8, 128), F32),
            pltpu.VMEM((4,) + gains[0].shape, F32),
            pltpu.VMEM((2, 8) + mine[0].shape, BF16),
            pltpu.VMEM((512, width), BF16),
            pltpu.VMEM((512, 256), F32),
            pltpu.SemaphoreType.DMA((8,)),
            pltpu.SemaphoreType.DMA((4,)),
            pltpu.SemaphoreType.DMA((8,)),
            pltpu.SemaphoreType.DMA((8,)),
        ],
        compiler_params=params(),
        cost_estimate=pl.CostEstimate(flops=2 * 512 * 8 * width * 256, bytes_accessed=6 * MIB, transcendentals=0),
        name="output",
    )(*raws, *others, *gains, *mine, *theirs, target)


def back_kernel(*refs):
    res_ref, own_refs, mine_refs, theirs_refs, out_ref = refs[0], refs[1:5], refs[5:13], refs[13:21], refs[21]
    first = lax.axis_index("core") == 0
    for k in range(4):
        for a in range(2):
            mine, theirs = mine_refs[a * 4 + k][...], theirs_refs[a * 4 + k][...]
            down = jnp.concatenate([jnp.where(first, mine, theirs), jnp.where(first, theirs, mine)], axis=1)
            raw = jnp.concatenate([own_refs[k][a, 0], own_refs[k][a, 1]])
            for at in range(0, 16, 8):
                res = res_ref[at : at + 8].reshape(256, 256)
                back = lax.dot_general(res, down, (((1,), (1,)), ((), ())), preferred_element_type=F32)
                out_ref[at : at + 8, a * 4 + k, :] = jnp.sum(back.reshape(8, 32, -1) * raw[None], axis=1)


def back_call(res, owns, mine, theirs):
    width = owns[0].shape[3]
    return pl.pallas_call(
        back_kernel,
        in_specs=[VMEM] * 21,
        out_specs=VMEM,
        out_shape=jax.ShapeDtypeStruct((16, 8, width), F32),
        compiler_params=params(),
        cost_estimate=pl.CostEstimate(flops=2 * 512 * 8 * width * 256, bytes_accessed=6 * MIB, transcendentals=0),
        name="back",
    )(res, *owns, *mine, *theirs)


def total_kernel(part_ref, out_ref):
    y, zh = lax.axis_index("y"), lax.axis_index("zh")
    total = jnp.sum(part_ref[...], axis=0)
    for a in range(2):
        for k in range(4):
            p = a * 4 + k
            at = (zh ^ a) * 4 + (y ^ k)
            out_ref[at] = jnp.zeros((8, 128), F32)
            for lane in range(total.shape[1] // 128):
                out_ref[at, lane : lane + 1, :] = total[p : p + 1, lane * 128 : lane * 128 + 128]


def total_call(part):
    return pl.pallas_call(
        total_kernel,
        in_specs=[VMEM],
        out_specs=VMEM,
        out_shape=jax.ShapeDtypeStruct((8, 8, 128), F32),
        compiler_params=params(),
        name="total",
    )(part)


def pair_kernel(near_ref, far_ref, *out_refs):
    for k in range(4):
        out_refs[k][0] = near_ref[k]
        out_refs[k][1] = far_ref[k]


def pair_call(near, far):
    return pl.pallas_call(
        pair_kernel,
        in_specs=[VMEM] * 2,
        out_specs=[VMEM] * 4,
        out_shape=[jax.ShapeDtypeStruct((2,) + near.shape[1:], F32)] * 4,
        compiler_params=params(),
        name="pair",
    )(near, far)


def hidden_kernel(gain_ref, *refs):
    mine_refs, other_refs, out_ref, block = refs[:4], refs[4:8], refs[8], refs[9]
    core, zh = lax.axis_index("core"), lax.axis_index("zh")
    gain = gain_ref[...]
    for k in range(4):
        for z in range(2):
            for e in range(2):
                raw = jnp.where(core == e, mine_refs[k][zh ^ z], other_refs[k][zh ^ z])
                at = (k * 2 + z) * 32 + e * 16
                block[at : at + 16, :] = (raw * gain).astype(BF16)
    out_ref[...] = block[...].T


def hidden_call(gain, mine, others):
    width = gain.shape[1]
    return pl.pallas_call(
        hidden_kernel,
        in_specs=[VMEM] * 9,
        out_specs=VMEM,
        out_shape=jax.ShapeDtypeStruct((width, 256), BF16),
        scratch_shapes=[pltpu.VMEM((256, width), BF16)],
        compiler_params=params(),
        name="hidden",
    )(gain, *mine, *others)


def grad_kernel(scale, hidden_ref, *refs):
    res_refs, out_ref, res_all, sem = refs[:4], refs[4], refs[5], refs[6]
    step = pl.program_id(0)
    some = out_ref.shape[2] // 256

    def copies(at):
        for k in range(4):
            for z in range(2):
                part = pl.ds(z * 16 + at * some, some)
                yield pltpu.make_async_copy(res_refs[k].at[part], res_all.at[k, part], sem.at[at, k * 2 + z])

    @pl.when(step == 0)
    def _():
        for at in range(16 // some):
            for copy in copies(at):
                copy.start()

    for copy in copies(step):
        copy.wait()

    block = jnp.concatenate(
        [
            jnp.concatenate([res_all[k, z * 16 + step * some + q] for k in range(4) for z in range(2)])
            for q in range(some)
        ],
        axis=1,
    )
    grad = jnp.dot(hidden_ref[...], block, preferred_element_type=F32)
    out_ref[0] = (grad * scale).astype(BF16)


def grad_call(hidden, res4, scale):
    width = hidden.shape[0]
    pieces, rows, feats = res4[0].shape
    blocks, some = pieces // 2, 4
    return pl.pallas_call(
        functools.partial(grad_kernel, scale),
        grid=(blocks // some,),
        in_specs=[pl.BlockSpec(hidden.shape, lambda s: (0, 0))] + [HBM] * 4,
        out_specs=pl.BlockSpec((1, width, some * feats), lambda s: (0, 0, s)),
        out_shape=jax.ShapeDtypeStruct((1, width, blocks * feats), BF16),
        scratch_shapes=[pltpu.VMEM((4, pieces, rows, feats), BF16), pltpu.SemaphoreType.DMA((blocks // some, 8))],
        compiler_params=params(),
        cost_estimate=pl.CostEstimate(
            flops=40 * 8 * rows * width * blocks * feats, bytes_accessed=10 * MIB, transcendentals=0
        ),
        name="grad",
    )(hidden, *res4)


def local(inputs, gate, up, down, targets, widths, gains):
    me = {a: lax.axis_index(a) for a in AXES}
    first = me["core"] == 0
    rows = inputs.shape[1]
    width = gate.shape[1]
    scale = 1.0 / rows**0.5

    theirs = swap(jnp.where(first, up, gate), "core")
    inputs_other = swap(inputs, "core")
    part, gain = part_call(inputs, inputs_other, gate, up, theirs, widths, gains, targets)
    down = after(down, part)
    part = lax.all_to_all(part, ("x", "y"), 0, 0, tiled=True)
    far = swap(down, "zh")
    part = sum_call(after(part, far))
    down, far = after((down, far), part)
    part = lax.all_to_all(part, ("zh", "zl"), 0, 0, tiled=True)
    mine = near4(down, "y")
    part = after(part, mine)
    raw, target, gain_z = raw_call(part, swap(part, "core"))
    mine, far = after((mine, far), raw)
    raw = lax.all_to_all(raw, "zl", 0, 0, tiled=True)
    theirs = [swap(d, "core") for d in mine]
    mine_far = near4(far, "y")
    raw = after(raw, (theirs, mine_far))
    raws = near4(raw, "x")
    others = [swap(r, "core") for r in raws]
    mine_far, gain_z = after((mine_far, gain_z), raw)
    theirs_far = [swap(d, "core") for d in mine_far]
    all_gains = near4(gain_z, "y")
    mine, theirs = mine + mine_far, theirs + theirs_far

    near, far = extract_call(raws, others)
    far = swap(far, "zh")
    raws, others = after((raws, others), near)

    res, *rows8 = output_call(raws, others, all_gains, mine, theirs, target)
    res_own = lax.all_to_all(after(res, far), ("zh", "zl", "x"), 0, 0, tiled=True)
    owns = pair_call(*after((near, far), res))
    got = [owns[0]] + [swap(owns[k], "y", k) for k in (1, 2, 3)]
    sums = back_call(after(res, owns), rows8, mine, theirs)
    res_own = after(res_own, (sums, got))
    res4 = near4(res_own, "y")
    sums, got = after((sums, got), res_own)
    sums = lax.all_to_all(sums, ("zl", "x"), 0, 0, tiled=True)
    hidden = hidden_call(gain, got, [swap(g, "core") for g in got])
    sums = lax.all_to_all(total_call(sums), ("zh", "y"), 0, 0, tiled=True)
    grad_down = grad_call(hidden, res4, scale)
    sums = jnp.sum(after(sums, grad_down), axis=0)[: width // 128].reshape(1, width)
    column = (me["zh"] * 4 + me["y"]) * width + lax.broadcasted_iota(jnp.int32, (1, width), 1)
    kept = (column < widths[0]).astype(F32)
    return grad_down, kept * sums * scale


def solution(mesh):
    fine = Mesh(mesh.devices.reshape(SHAPE), AXES)
    tp = ("zh", "y")
    return jax.shard_map(
        local,
        mesh=fine,
        in_specs=(P(VAR, None), P(VAR, tp), P(VAR, tp), P(tp, VAR), P(VAR, tp), P(VAR), P(VAR, tp)),
        out_specs=(P(VAR, tp, None), P(VAR, tp)),
        check_vma=False,
    )
```

```python
import functools

import jax
import jax.numpy as jnp
from jax import lax
from jax.experimental import pallas as pl
from jax.experimental.pallas import tpu as pltpu
from jax.sharding import Mesh, PartitionSpec as P

SHAPE = (4, 4, 2, 2, 4)
AXES = ("zl", "x", "core", "zh", "y")
VAR = ("zl", "x", "core")
SIZE = dict(zip(AXES, SHAPE))
MIB = 1024 * 1024
F32, BF16 = jnp.float32, jnp.bfloat16


def swap(value, axis, mask=1):
    if mask == 0:
        return value
    return lax.ppermute(value, axis, [(i, i ^ mask) for i in range(SIZE[axis])])


def near4(value, axis):
    return [value] + [swap(value, axis, k) for k in (1, 2, 3)]


def after(value, other):
    return lax.optimization_barrier((value, other))[0]


def params(mib):
    return pltpu.CompilerParams(vmem_limit_bytes=mib * MIB)


SMEM = pl.BlockSpec(memory_space=pltpu.SMEM)
VMEM = pl.BlockSpec(memory_space=pltpu.VMEM)
HBM = pl.BlockSpec(memory_space=pl.ANY)


def part_kernel(x_ref, x_other_ref, gate_ref, up_ref, theirs_ref, width_ref, gains_ref, target_ref, out_ref, gain_ref):
    core = lax.axis_index("core")
    lanes = gate_ref.shape[1] // 128
    mine = jnp.where(core == 0, gate_ref[...], up_ref[...])
    x = jnp.concatenate([x_ref[...], x_other_ref[...]]).T
    part = jnp.dot(x, jnp.concatenate([mine, theirs_ref[...]]), preferred_element_type=F32)
    target = target_ref[...].astype(F32)
    width = gate_ref.shape[1]
    column = (lax.axis_index("zh") * 4 + lax.axis_index("y")) * width + lax.broadcasted_iota(jnp.int32, (1, width), 1)
    gain = jnp.where(column < width_ref[0], gains_ref[...], 0.0)
    gain_ref[...] = gain
    for slot in range(16):
        for e in range(2):
            for lane in range(lanes):
                at = slot * 16 + e * 8
                out_ref[slot, e * lanes + lane] = part[at : at + 8, lane * 128 : lane * 128 + 128]
        for half in range(2):
            at = ((slot // 4) % 2) * 256 + half * 128
            out_ref[slot, 2 * lanes + half] = target[:, at : at + 128]
        out_ref[slot, 2 * lanes + 2] = jnp.zeros((8, 128), F32)
        for lane in range(lanes):
            out_ref[slot, 2 * lanes + 2, lane : lane + 1, :] = gain[:, lane * 128 : lane * 128 + 128]


def part_call(x, x_other, gate, up, theirs, widths, gains, targets):
    lanes = gate.shape[1] // 128
    return pl.pallas_call(
        part_kernel,
        in_specs=[VMEM] * 5 + [SMEM] + [VMEM] * 2,
        out_specs=[VMEM] * 2,
        out_shape=[
            jax.ShapeDtypeStruct((16, 2 * lanes + 3, 8, 128), F32),
            jax.ShapeDtypeStruct(gains.shape, F32),
        ],
        compiler_params=params(56),
        name="part",
    )(x, x_other, gate, up, theirs, widths, gains, targets)


def sum_kernel(part_ref, out_ref, held, sem):
    lanes = out_ref.shape[1] - 6
    copies = [
        pltpu.make_async_copy(part_ref.at[i * 4 + y], held.at[i * 4 + y], sem.at[i * 4 + y])
        for y in range(4)
        for i in range(4)
    ]
    for copy in copies:
        copy.start()
    for y in range(4):
        for copy in copies[y * 4 : y * 4 + 4]:
            copy.wait()
        for e in range(2):
            for lane in range(lanes):
                t = e * lanes + lane
                total = (held[y, t] + held[4 + y, t]) + (held[8 + y, t] + held[12 + y, t])
                out_ref[:, lane, y * 2 + e, :] = total
    x, y = lax.axis_index("x"), lax.axis_index("y")
    for high in range(2):
        for half in range(2):
            target = held[y * 4 + high * 2 + x // 2, 2 * lanes + half]
            for slot in range(high, 8, 2):
                out_ref[slot, lanes + half] = target
    for k in range(4):
        gain = held[k * 4 + y, 2 * lanes + 2]
        for slot in range(8):
            out_ref[slot, lanes + 2 + k] = gain


def sum_call(part):
    lanes = (part.shape[1] - 3) // 2
    return pl.pallas_call(
        sum_kernel,
        in_specs=[HBM],
        out_specs=VMEM,
        out_shape=jax.ShapeDtypeStruct((8, lanes + 6, 8, 128), F32),
        scratch_shapes=[pltpu.VMEM(part.shape, F32), pltpu.SemaphoreType.DMA((16,))],
        compiler_params=params(8),
        name="sum_x",
    )(part)


def raw_kernel(mine_ref, other_ref, out_ref, target_ref, gain_ref):
    first = lax.axis_index("core") == 0
    lanes = out_ref.shape[1]
    unit = lax.axis_index("core") * 4
    for lane in range(lanes):
        mine, other = (
            (r[unit, lane] + r[unit + 1, lane]) + (r[unit + 2, lane] + r[unit + 3, lane]) for r in (mine_ref, other_ref)
        )
        raw = jax.nn.silu(jnp.where(first, mine, other)) * jnp.where(first, other, mine)
        for copy in range(4):
            out_ref[copy, lane] = raw
    gain_ref[...] = mine_ref[:, lanes + 2 :]
    source, row = (lax.axis_index("zl") // 2) * 4, lax.axis_index("zh")
    for half in range(2):
        cols = slice(half * 128, half * 128 + 128)
        for x in range(4):
            own, far = mine_ref[source + x, lanes + half], other_ref[source + x, lanes + half]
            for e in range(2):
                target = jnp.where(first == (e == 0), own, far)
                target_ref[e, x * 4 : x * 4 + 4, cols] = jnp.where(row == 0, target[:4], target[4:])


def raw_call(mine, other):
    lanes = mine.shape[1] - 6
    return pl.pallas_call(
        raw_kernel,
        in_specs=[VMEM, VMEM],
        out_specs=[VMEM] * 3,
        out_shape=[
            jax.ShapeDtypeStruct((4, lanes, 8, 128), F32),
            jax.ShapeDtypeStruct((2, 16, 256), F32),
            jax.ShapeDtypeStruct((8, 4, 8, 128), F32),
        ],
        compiler_params=params(6),
        name="raw",
    )(mine, other)


def extract_kernel(*refs):
    x, core, y, zh = (lax.axis_index(a) for a in ("x", "core", "y", "zh"))
    raw_refs, other_refs, out_refs, both = refs[:4], refs[4:8], refs[8:10], refs[10]
    for k in range(4):
        at = pl.ds((x ^ k) * 4, 4)
        both[core, at] = raw_refs[k][...]
        both[1 - core, at] = other_refs[k][...]
    for a in range(2):
        for k in range(4):
            for lane in range(both.shape[2]):
                out_refs[a][k, :, lane * 128 : lane * 128 + 128] = both[zh ^ a, :, lane, (y ^ k) * 2 + core, :]


def extract_call(raws, others):
    lanes = raws[0].shape[1]
    return pl.pallas_call(
        extract_kernel,
        in_specs=[VMEM] * 8,
        out_specs=[VMEM] * 2,
        out_shape=[jax.ShapeDtypeStruct((4, 16, lanes * 128), F32)] * 2,
        scratch_shapes=[pltpu.VMEM((2, 16, lanes, 8, 128), F32)],
        compiler_params=params(8),
        name="extract",
    )(*raws, *others)


def output_kernel(*refs):
    raw_refs, other_refs, gain_refs, mine_refs, theirs_refs = refs[:4], refs[4:8], refs[8:12], refs[12:20], refs[20:28]
    target_ref, res_ref, row_refs = refs[28], refs[29], refs[30:34]
    raw_all, gain_all, down_all, hidden, total, raw_sem, gain_sem, mine_sem, theirs_sem = refs[34:]
    x, core, y, zh = (lax.axis_index(a) for a in ("x", "core", "y", "zh"))
    lanes = raw_all.shape[2]
    first, second = [], []
    for k in range(4):
        at = pl.ds((x ^ k) * 4, 4)
        first.append(pltpu.make_async_copy(raw_refs[k], raw_all.at[core, at], raw_sem.at[k]))
        first.append(pltpu.make_async_copy(other_refs[k], raw_all.at[1 - core, at], raw_sem.at[4 + k]))
        first.append(pltpu.make_async_copy(gain_refs[k], gain_all.at[y ^ k], gain_sem.at[k]))
    for p in range(8):
        second.append(pltpu.make_async_copy(mine_refs[p], down_all.at[core, p], mine_sem.at[p]))
        second.append(pltpu.make_async_copy(theirs_refs[p], down_all.at[1 - core, p], theirs_sem.at[p]))
    for copy in first + second:
        copy.start()
    for copy in first:
        copy.wait()
    for p in range(8):
        second[2 * p].wait()
        second[2 * p + 1].wait()
        a, k = p // 4, p % 4
        unit, other = zh ^ a, y ^ k
        for lane in range(lanes):
            cols = slice(lane * 128, lane * 128 + 128)
            for e in range(2):
                raw = raw_all[unit, :, lane, other * 2 + e, :]
                row_refs[k][a, e, :, cols] = raw
                for v in range(16):
                    gain = gain_all[other, unit * 4 + v // 4, v % 4, lane : lane + 1, :]
                    at = v * 32 + e * 16
                    hidden[at : at + 16, cols] = (raw * gain).astype(BF16)
        down = jnp.concatenate([down_all[0, p], down_all[1, p]], axis=1)
        term = jnp.dot(hidden[...], down, preferred_element_type=F32)
        if p == 0:
            total[...] = term
        else:
            total[...] += term
    for e in range(2):
        target = target_ref[e]
        for v in range(16):
            at = v * 32 + e * 16
            res = (total[at : at + 16, :] - target).astype(BF16)
            for copy in range(2):
                res_ref[copy * 16 + v, e * 16 : e * 16 + 16, :] = res


def output_call(raws, others, gains, mine, theirs, target):
    lanes = raws[0].shape[1]
    width = lanes * 128
    return pl.pallas_call(
        output_kernel,
        in_specs=[HBM] * 28 + [VMEM],
        out_specs=[VMEM] * 5,
        out_shape=[jax.ShapeDtypeStruct((32, 32, 256), BF16)]
        + [jax.ShapeDtypeStruct((2, 2, 16, width), F32)] * 4,
        scratch_shapes=[
            pltpu.VMEM((2, 16, lanes, 8, 128), F32),
            pltpu.VMEM((4,) + gains[0].shape, F32),
            pltpu.VMEM((2, 8) + mine[0].shape, BF16),
            pltpu.VMEM((512, width), BF16),
            pltpu.VMEM((512, 256), F32),
            pltpu.SemaphoreType.DMA((8,)),
            pltpu.SemaphoreType.DMA((4,)),
            pltpu.SemaphoreType.DMA((8,)),
            pltpu.SemaphoreType.DMA((8,)),
        ],
        compiler_params=params(56),
        cost_estimate=pl.CostEstimate(flops=2 * 512 * 8 * width * 256, bytes_accessed=6 * MIB, transcendentals=0),
        name="output",
    )(*raws, *others, *gains, *mine, *theirs, target)


def back_kernel(*refs):
    res_ref, own_refs, mine_refs, theirs_refs, out_ref = refs[0], refs[1:5], refs[5:13], refs[13:21], refs[21]
    first = lax.axis_index("core") == 0
    for k in range(4):
        for a in range(2):
            mine, theirs = mine_refs[a * 4 + k][...], theirs_refs[a * 4 + k][...]
            down = jnp.concatenate([jnp.where(first, mine, theirs), jnp.where(first, theirs, mine)], axis=1)
            raw = jnp.concatenate([own_refs[k][a, 0], own_refs[k][a, 1]])
            for at in range(0, 16, 8):
                res = res_ref[at : at + 8].reshape(256, 256)
                back = lax.dot_general(res, down, (((1,), (1,)), ((), ())), preferred_element_type=F32)
                out_ref[at : at + 8, a * 4 + k, :] = jnp.sum(back.reshape(8, 32, -1) * raw[None], axis=1)


def back_call(res, owns, mine, theirs):
    width = owns[0].shape[3]
    return pl.pallas_call(
        back_kernel,
        in_specs=[VMEM] * 21,
        out_specs=VMEM,
        out_shape=jax.ShapeDtypeStruct((16, 8, width), F32),
        compiler_params=params(56),
        cost_estimate=pl.CostEstimate(flops=2 * 512 * 8 * width * 256, bytes_accessed=6 * MIB, transcendentals=0),
        name="back",
    )(res, *owns, *mine, *theirs)


def total_kernel(part_ref, out_ref):
    y, zh = lax.axis_index("y"), lax.axis_index("zh")
    total = jnp.sum(part_ref[...], axis=0)
    for a in range(2):
        for k in range(4):
            p = a * 4 + k
            at = (zh ^ a) * 4 + (y ^ k)
            out_ref[at] = jnp.zeros((8, 128), F32)
            for lane in range(total.shape[1] // 128):
                out_ref[at, lane : lane + 1, :] = total[p : p + 1, lane * 128 : lane * 128 + 128]


def total_call(part):
    return pl.pallas_call(
        total_kernel,
        in_specs=[VMEM],
        out_specs=VMEM,
        out_shape=jax.ShapeDtypeStruct((8, 8, 128), F32),
        compiler_params=params(6),
        name="total",
    )(part)


def pair_kernel(near_ref, far_ref, *out_refs):
    for k in range(4):
        out_refs[k][0] = near_ref[k]
        out_refs[k][1] = far_ref[k]


def pair_call(near, far):
    return pl.pallas_call(
        pair_kernel,
        in_specs=[VMEM] * 2,
        out_specs=[VMEM] * 4,
        out_shape=[jax.ShapeDtypeStruct((2,) + near.shape[1:], F32)] * 4,
        compiler_params=params(6),
        name="pair",
    )(near, far)


def hidden_kernel(gain_ref, *refs):
    mine_refs, other_refs, out_ref, block = refs[:4], refs[4:8], refs[8], refs[9]
    core, zh = lax.axis_index("core"), lax.axis_index("zh")
    gain = gain_ref[...]
    for k in range(4):
        for z in range(2):
            for e in range(2):
                raw = jnp.where(core == e, mine_refs[k][zh ^ z], other_refs[k][zh ^ z])
                at = (k * 2 + z) * 32 + e * 16
                block[at : at + 16, :] = (raw * gain).astype(BF16)
    out_ref[...] = block[...].T


def hidden_call(gain, mine, others):
    width = gain.shape[1]
    return pl.pallas_call(
        hidden_kernel,
        in_specs=[VMEM] * 9,
        out_specs=VMEM,
        out_shape=jax.ShapeDtypeStruct((width, 256), BF16),
        scratch_shapes=[pltpu.VMEM((256, width), BF16)],
        compiler_params=params(8),
        name="hidden",
    )(gain, *mine, *others)


def grad_kernel(scale, hidden_ref, *refs):
    res_refs, out_ref, res_all, sem = refs[:4], refs[4], refs[5], refs[6]
    step = pl.program_id(0)
    some = out_ref.shape[2] // 256

    def copies(at):
        for k in range(4):
            for z in range(2):
                part = pl.ds(z * 16 + at * some, some)
                yield pltpu.make_async_copy(res_refs[k].at[part], res_all.at[k, part], sem.at[at, k * 2 + z])

    @pl.when(step == 0)
    def _():
        for at in range(16 // some):
            for copy in copies(at):
                copy.start()

    for copy in copies(step):
        copy.wait()

    block = jnp.concatenate(
        [
            jnp.concatenate([res_all[k, z * 16 + step * some + q] for k in range(4) for z in range(2)])
            for q in range(some)
        ],
        axis=1,
    )
    grad = jnp.dot(hidden_ref[...], block, preferred_element_type=F32)
    out_ref[0] = (grad * scale).astype(BF16)


def grad_call(hidden, res4, scale):
    width = hidden.shape[0]
    pieces, rows, feats = res4[0].shape
    blocks, some = pieces // 2, 4
    return pl.pallas_call(
        functools.partial(grad_kernel, scale),
        grid=(blocks // some,),
        in_specs=[pl.BlockSpec(hidden.shape, lambda s: (0, 0))] + [HBM] * 4,
        out_specs=pl.BlockSpec((1, width, some * feats), lambda s: (0, 0, s)),
        out_shape=jax.ShapeDtypeStruct((1, width, blocks * feats), BF16),
        scratch_shapes=[pltpu.VMEM((4, pieces, rows, feats), BF16), pltpu.SemaphoreType.DMA((blocks // some, 8))],
        compiler_params=params(22),
        cost_estimate=pl.CostEstimate(
            flops=40 * 8 * rows * width * blocks * feats, bytes_accessed=10 * MIB, transcendentals=0
        ),
        name="grad",
    )(hidden, *res4)


def local(inputs, gate, up, down, targets, widths, gains):
    me = {a: lax.axis_index(a) for a in AXES}
    first = me["core"] == 0
    rows = inputs.shape[1]
    width = gate.shape[1]
    scale = 1.0 / rows**0.5

    theirs = swap(jnp.where(first, up, gate), "core")
    inputs_other = swap(inputs, "core")
    part, gain = part_call(inputs, inputs_other, gate, up, theirs, widths, gains, targets)
    down = after(down, part)
    part = lax.all_to_all(part, ("x", "y"), 0, 0, tiled=True)
    far = swap(down, "zh")
    part = sum_call(after(part, far))
    down, far = after((down, far), part)
    part = lax.all_to_all(part, ("zh", "zl"), 0, 0, tiled=True)
    mine = near4(down, "y")
    part = after(part, mine)
    raw, target, gain_z = raw_call(part, swap(part, "core"))
    mine, far = after((mine, far), raw)
    raw = lax.all_to_all(raw, "zl", 0, 0, tiled=True)
    theirs = [swap(d, "core") for d in mine]
    mine_far = near4(far, "y")
    raw = after(raw, (theirs, mine_far))
    raws = near4(raw, "x")
    others = [swap(r, "core") for r in raws]
    mine_far, gain_z = after((mine_far, gain_z), raw)
    theirs_far = [swap(d, "core") for d in mine_far]
    all_gains = near4(gain_z, "y")
    mine, theirs = mine + mine_far, theirs + theirs_far

    near, far = extract_call(raws, others)
    far = swap(far, "zh")
    raws, others = after((raws, others), near)

    res, *rows8 = output_call(raws, others, all_gains, mine, theirs, target)
    res_own = lax.all_to_all(after(res, far), ("zh", "zl", "x"), 0, 0, tiled=True)
    owns = pair_call(*after((near, far), res))
    got = [owns[0]] + [swap(owns[k], "y", k) for k in (1, 2, 3)]
    sums = back_call(after(res, owns), rows8, mine, theirs)
    res_own = after(res_own, (sums, got))
    res4 = near4(res_own, "y")
    sums, got = after((sums, got), res_own)
    sums = lax.all_to_all(sums, ("zl", "x"), 0, 0, tiled=True)
    hidden = hidden_call(gain, got, [swap(g, "core") for g in got])
    sums = lax.all_to_all(total_call(sums), ("zh", "y"), 0, 0, tiled=True)
    grad_down = grad_call(hidden, res4, scale)
    sums = jnp.sum(after(sums, grad_down), axis=0)[: width // 128].reshape(1, width)
    column = (me["zh"] * 4 + me["y"]) * width + lax.broadcasted_iota(jnp.int32, (1, width), 1)
    kept = (column < widths[0]).astype(F32)
    return grad_down, kept * sums * scale


def solution(mesh):
    fine = Mesh(mesh.devices.reshape(SHAPE), AXES)
    tp = ("zh", "y")
    return jax.shard_map(
        local,
        mesh=fine,
        in_specs=(P(VAR, None), P(VAR, tp), P(VAR, tp), P(tp, VAR), P(VAR, tp), P(VAR), P(VAR, tp)),
        out_specs=(P(VAR, tp, None), P(VAR, tp)),
        check_vma=False,
    )
```
